32 devices in a mesh: grp: 2 (over x), reg: 16 (over z, y, core).
Axes of the slice: x: 2, y: 2, z: 4, core: 2. Of those that a mesh axis runs over, the one named last changes fastest.
Arguments:
- field: float32 [8, 137, 32768], P('grp', None, 'reg'), parts along dimension 0, may hold values from -6 to 6
- stencil: int32 [3, 32768], P(None, 'reg'), may hold values from 0 to 2559, as said below
- weights: float32 [3, 32768], P(None, 'reg'), may hold values from 0.2 to 1
- counts: int32 [16], replicated, may hold values from 2 to 16, as said below
- geometry: float32 [3, 32768], replicated, as said below
- vertical: float32 [137, 137], replicated, as said below
Outputs:
- control: float32 [8, 137, 32768], P('grp', None, 'reg'), parts along dimension 0
The draws below stay inside these ranges and needn't reach their ends.
There are 2 independent parts, one for each index of `grp`. The reference program is written for one: setup_inputs(seed, part) draws one part's arguments, and reference() takes and returns one part's arrays. A program takes and returns all parts, laid end to end along the dimension named above; an argument that names none is the same for every part. Nothing has to cross between parts.
Inputs may be any that keep to these rules, and one draw needn't show every extreme that they name: `counts`: every region has between 2 and 16 live tiles; some region has exactly 16 and some exactly 2. `stencil`: codes name only live slots of the named region. `geometry`: supports lie between 0.15 and 0.4; x of live slots lies in [0, 1). `vertical`: entries farther than 6 from the diagonal are zero.
All inputs are finite; a program needn't handle non-finite values.
Results may differ from the reference program's by a relative error of at most 0.0035.
Values may be sent and summed in bfloat16 or wider, within the bound.
A program may use at most 128 MiB of HBM per device.

```python
import jax
import jax.numpy as jnp
from jax import lax

MEM = 4
LEV = 137
CELLS_DEV = 2048
TILES_DEV = 16
TILE = 128
EDGE = 2
STENCIL = 3
BAND = 6
REGIONS = 16
CELLS = 32768
SUB = 32768


def shared_counts(key):
    first_key, second_key, third_key, fourth_key = jax.random.split(key, 4)
    spread = TILES_DEV - EDGE
    first_draw = jax.random.randint(first_key, (REGIONS,), 0, spread + 1)
    second_draw = jax.random.randint(second_key, (REGIONS,), 0, spread + 1)
    tiles_live = EDGE + first_draw * second_draw // max(spread, 1)
    busiest = jax.random.randint(third_key, (), 0, REGIONS)
    tiles_live = tiles_live.at[busiest].set(TILES_DEV)
    lightest = (busiest + 1 + jax.random.randint(fourth_key, (), 0, REGIONS - 1)) % REGIONS
    tiles_live = tiles_live.at[lightest].set(EDGE)
    return tiles_live.astype(jnp.int32)


def draw_counts(key, part):
    return shared_counts(key)


def draw_stencil(key, part):
    tiles_live = shared_counts(key)
    key = jax.random.fold_in(key, 7)
    kind_key, own_key, rim_key = jax.random.split(key, 3)
    subset_rows = TILES_DEV * TILE
    rim_rows = EDGE * TILE
    region = jnp.arange(CELLS) // CELLS_DEV
    kinds = jax.random.randint(kind_key, (STENCIL, CELLS), 0, 10)
    own_rows = jax.random.randint(own_key, (STENCIL, CELLS), 0, 1 << 20) % (tiles_live[region] * TILE)[None, :]
    rim_pick = jax.random.randint(rim_key, (STENCIL, CELLS), 0, rim_rows)
    codes = jnp.where(kinds == 0, rim_pick, jnp.where(kinds == 1, rim_rows + subset_rows + rim_pick, rim_rows + own_rows))
    codes = codes.at[0, 0].set(0)
    codes = codes.at[1, 0].set(2 * rim_rows + subset_rows - 1)
    return codes.astype(jnp.int32)


def draw_geometry(key, part):
    tiles_live = shared_counts(key)
    key = jax.random.fold_in(key, 11)
    x_key, y_key, support_key = jax.random.split(key, 3)
    subset_rows = TILES_DEV * TILE
    slot = jnp.arange(SUB)
    region = slot // subset_rows
    tile_index = slot % subset_rows // TILE
    uniform_x = jax.random.uniform(x_key, (SUB,), jnp.float32)
    x_position = (tile_index.astype(jnp.float32) + uniform_x) / tiles_live[region].astype(jnp.float32)
    y_position = 0.25 * jax.random.uniform(y_key, (SUB,), jnp.float32)
    support = jnp.exp(jax.random.uniform(support_key, (SUB,), jnp.float32, minval=jnp.log(0.15), maxval=jnp.log(0.4)))
    return jnp.stack([x_position, y_position, support]).astype(jnp.float32)


def draw_vertical(key, part):
    key = jax.random.fold_in(key, 13)
    levels_index = jnp.arange(LEV)
    spacing = jnp.abs(levels_index[:, None] - levels_index[None, :])
    values = jax.random.uniform(key, (LEV, LEV), jnp.float32, minval=0.1, maxval=0.5)
    banded = jnp.where(spacing == 0, 1.0, jnp.where(spacing <= BAND, values, 0.0))
    return (banded / (1.0 + 0.6 * BAND)).astype(jnp.float32)


def shard_levels(key, extent, pieces, smallest, high):
    gain = 1.0
    for axis_at, shards_of in pieces:
        steps = jax.random.uniform(jax.random.fold_in(jax.random.fold_in(key, 6), axis_at), (shards_of,), jnp.float32, smallest / len(pieces), high / len(pieces))
        gain = gain * jnp.repeat(jnp.exp(steps), extent[axis_at] // shards_of).reshape((-1,) + (1,) * (len(extent) - 1 - axis_at))
    return gain


def normal_values(rng, shape, deviation, most, cuts=(), held_as=jnp.bfloat16):
    drawn = deviation * jax.random.normal(rng, shape, jnp.float32)
    if cuts:
        drawn = drawn * shard_levels(rng, shape, cuts, -0.22, 0.18)
    return jnp.clip(drawn, -most, most).astype(held_as)


def setup_inputs(seed: int = 0, part: int = 0) -> dict:
    splits = jax.random.split(jax.random.key(seed), 7)
    part_splits = jax.random.split(jax.random.fold_in(splits[6], part), 7)
    return {
        "field": normal_values(part_splits[0], (MEM, LEV, CELLS), 1.0, 6.0, ((2, 16),), jnp.float32),
        "stencil": draw_stencil(jax.random.fold_in(splits[6], 71), part),
        "weights": jnp.clip(0.2 + 0.8 * jax.random.uniform(splits[2], (STENCIL, CELLS), jnp.float32) ** shard_levels(splits[2], (STENCIL, CELLS), ((1, 16),), -0.2, 0.2), 0.2, 1.0),
        "counts": draw_counts(jax.random.fold_in(splits[6], 71), part),
        "geometry": draw_geometry(jax.random.fold_in(splits[6], 71), part),
        "vertical": draw_vertical(jax.random.fold_in(splits[6], 71), part),
    }


def kernel_block(row_geometry, column_geometry):
    delta_x = row_geometry[0][:, None] - column_geometry[0][None, :]
    delta_y = row_geometry[1][:, None] - column_geometry[1][None, :]
    distance = jnp.sqrt(delta_x * delta_x + delta_y * delta_y)
    ratio = distance / (0.5 * (row_geometry[2][:, None] + column_geometry[2][None, :]))
    base_term = jnp.maximum(1.0 - ratio, 0.0)
    return (base_term * base_term * base_term * base_term * (1.0 + 4.0 * ratio)).astype(jnp.bfloat16)

def reference(field, stencil, weights, counts, geometry, vertical):
    subset_rows = TILES_DEV * TILE
    rim_rows = EDGE * TILE
    flat_rows = MEM * LEV
    region = (jnp.arange(CELLS) // CELLS_DEV).astype(jnp.int32)
    lower_region = (region - 1) % REGIONS
    upper_region = (region + 1) % REGIONS
    columns = field.reshape(flat_rows, CELLS).T
    totals = jnp.zeros((SUB, flat_rows), jnp.float32)
    for stencil_slot in range(STENCIL):
        stencil_code = stencil[stencil_slot]
        own_target = region * subset_rows + stencil_code - rim_rows
        lower_target = lower_region * subset_rows + (counts[lower_region] - EDGE) * TILE + stencil_code
        upper_target = upper_region * subset_rows + stencil_code - rim_rows - subset_rows
        target = jnp.where(stencil_code < rim_rows, lower_target, jnp.where(stencil_code < rim_rows + subset_rows, own_target, upper_target))
        totals = totals + jax.ops.segment_sum(columns * weights[stencil_slot][:, None], target.astype(jnp.int32), num_segments=SUB)
    gathered = totals.T.reshape(MEM, LEV, SUB)
    smoothed = jnp.einsum('ij,mjs->mis', vertical, gathered, precision=lax.Precision.HIGHEST).astype(jnp.bfloat16)
    offset = jnp.array([[1.0], [0.0], [0.0]], dtype=geometry.dtype)

    def one_region(region_index):
        lower_index = (region_index - 1) % REGIONS
        upper_index = (region_index + 1) % REGIONS
        lower_start = (lower_index * subset_rows + (counts[lower_index] - EDGE) * TILE).astype(jnp.int32)
        own_start = (region_index * subset_rows).astype(jnp.int32)
        upper_start = (upper_index * subset_rows).astype(jnp.int32)
        values = jnp.concatenate([lax.dynamic_slice_in_dim(smoothed, lower_start, rim_rows, 2), lax.dynamic_slice_in_dim(smoothed, own_start, subset_rows, 2), lax.dynamic_slice_in_dim(smoothed, upper_start, rim_rows, 2)], axis=2)
        row_geometry = lax.dynamic_slice_in_dim(geometry, own_start, subset_rows, 1)
        column_geometry = jnp.concatenate([lax.dynamic_slice_in_dim(geometry, lower_start, rim_rows, 1) - offset, row_geometry, lax.dynamic_slice_in_dim(geometry, upper_start, rim_rows, 1) + offset], axis=1)
        kernel = kernel_block(row_geometry, column_geometry).astype(jnp.float32)
        product = jnp.dot(values.astype(jnp.float32).reshape(flat_rows, -1), kernel.T, precision=lax.Precision.HIGHEST)
        active = jnp.arange(subset_rows) < counts[region_index] * TILE
        return jnp.where(active[None, :], product, 0.0)
    outputs = lax.map(one_region, jnp.arange(REGIONS, dtype=jnp.int32))
    return outputs.reshape(REGIONS, MEM, LEV, subset_rows).transpose(1, 2, 0, 3).reshape(MEM, LEV, SUB)
```

```python
import functools

import jax
import jax.numpy as jnp
from jax import lax
from jax.experimental import pallas as pl
from jax.experimental.pallas import tpu as pltpu
from jax.sharding import PartitionSpec as P

TILES_DEV = 16
TILE = 128
EDGE = 2
BLOCK = EDGE * TILE
OWN_BLOCKS = TILES_DEV // EDGE
MESH = pl.DeviceIdType.MESH
NT = (((1,), (1,)), ((), ()))
NN = (((1,), (0,)), ((), ()))


def scatter_kernel(
    region_total,
    padded,
    stencil_ref,
    weights_ref,
    counts_ref,
    vertical_ref,
    field_ref,
    out_ref,
    columns,
    banded,
    inputs,
    onehot_even,
    onehot_odd,
    first_sum,
    tail_sum,
    ready,
    from_lower,
    from_upper,
    chunk_sems,
    out_sems,
    send_sems,
    recv_sems,
):
    members, levels, cells = field_ref.shape
    chunk = BLOCK
    chunks = cells // chunk
    me = lax.axis_index("reg")
    lower = lax.rem(me + region_total - 1, region_total)
    upper = lax.rem(me + 1, region_total)

    def chunk_copy(i):
        at = pl.ds(i * chunk, chunk)
        return pltpu.make_async_copy(
            field_ref.at[:, :, at], inputs.at[:, :, at], chunk_sems.at[i]
        )

    for i in range(chunks):
        chunk_copy(i).start()

    barrier = pltpu.get_barrier_semaphore()
    for neighbour in (lower, upper):
        pl.semaphore_signal(barrier, inc=1, device_id={"reg": neighbour}, device_id_type=MESH)

    tail_tile = counts_ref[me] - EDGE

    matrix = vertical_ref[...]
    high = matrix.astype(jnp.bfloat16)
    low = (matrix - high.astype(jnp.float32)).astype(jnp.bfloat16)
    banded[...] = jnp.zeros_like(banded)
    banded[0:levels, :] = high
    banded[padded : padded + levels, :] = low

    codes = [stencil_ref[k : k + 1, :] for k in range(3)]
    raw = [weights_ref[k : k + 1, :] for k in range(3)]
    merged = []
    for k in range(3):
        total = raw[k]
        for other in range(3):
            if other != k:
                total = total + jnp.where(codes[other] == codes[k], raw[other], 0.0)
        merged.append(total.astype(jnp.bfloat16))
    row_index = lax.broadcasted_iota(jnp.int32, (BLOCK, TILE), 0)
    row_index = row_index.astype(jnp.float32).astype(jnp.bfloat16)

    def make_onehot(target, base):
        wanted = []
        for k in range(3):
            shift = codes[k] - base
            inside = (shift >= 0) & (shift < BLOCK)
            shift = jnp.where(inside, shift, -1).astype(jnp.float32)
            wanted.append(shift.astype(jnp.bfloat16))
        for c in range(cells // TILE):
            at = slice(c * TILE, (c + 1) * TILE)
            value = jnp.zeros((BLOCK, TILE), jnp.bfloat16)
            for k in range(3):
                code = jnp.broadcast_to(wanted[k][:, at], (BLOCK, TILE))
                weight = jnp.broadcast_to(merged[k][:, at], (BLOCK, TILE))
                value = jnp.where(row_index == code, weight, value)
            target[:, at] = value

    def scattered(source):
        return lax.dot_general(
            columns[...], source[...], NT, preferred_element_type=jnp.float32
        )

    own = BLOCK
    bases = [0, BLOCK + OWN_BLOCKS * BLOCK, own, own + tail_tile * TILE]
    bases += [own + b * BLOCK for b in range(1, OWN_BLOCKS)]
    slots = [onehot_even, onehot_odd]
    make_onehot(slots[0], bases[0])

    for i in range(chunks):
        chunk_copy(i).wait()
        at = slice(i * chunk, (i + 1) * chunk)
        for m in range(members):
            part = inputs[m, :, at]
            part_high = part.astype(jnp.bfloat16)
            part_low = (part - part_high.astype(jnp.float32)).astype(jnp.bfloat16)
            both = jnp.dot(banded[...], part_high, preferred_element_type=jnp.float32)
            rest = jnp.dot(banded[0:padded, :], part_low, preferred_element_type=jnp.float32)
            value = both[0:padded] + (both[padded : 2 * padded] + rest)
            columns[m * padded : (m + 1) * padded, at] = value.astype(jnp.bfloat16)

    def remote(index, source, target, neighbour):
        return pltpu.make_async_remote_copy(
            src_ref=source,
            dst_ref=target,
            send_sem=send_sems.at[index],
            recv_sem=recv_sems.at[index],
            device_id={"reg": neighbour},
            device_id_type=MESH,
        )

    upper_at = EDGE + TILES_DEV
    tail_at = upper_at + EDGE
    give_lower = remote(0, ready.at[pl.ds(0, EDGE)], from_upper, lower)
    give_upper = remote(1, ready.at[pl.ds(upper_at, EDGE)], from_lower, upper)
    first_out = remote(2, ready.at[pl.ds(EDGE, EDGE)], out_ref.at[pl.ds(upper_at, EDGE)], lower)
    tail_out = remote(3, ready.at[pl.ds(tail_at, EDGE)], out_ref.at[pl.ds(0, EDGE)], upper)

    def local_out(index, tile):
        at = pl.ds(tile, EDGE)
        return pltpu.make_async_copy(ready.at[at], out_ref.at[at], out_sems.at[index])

    def put(tile, value):
        for half in range(EDGE):
            ready[tile + half] = value[:, half * TILE : (half + 1) * TILE].astype(jnp.bfloat16)

    def finish_edges():
        give_lower.wait_recv()
        give_upper.wait_recv()
        low0, low1 = from_lower[0].astype(jnp.float32), from_lower[1].astype(jnp.float32)
        up0, up1 = from_upper[0].astype(jnp.float32), from_upper[1].astype(jnp.float32)
        same = jnp.where(tail_tile == 0, 1.0, 0.0)
        next_one = jnp.where(tail_tile == 1, 1.0, 0.0)
        first_sum[:, 0:TILE] += low0 + same * up0
        first_sum[:, TILE:] += low1 + same * up1 + next_one * up0
        tail_sum[:, 0:TILE] += up0 + same * low0 + next_one * low1
        tail_sum[:, TILE:] += up1 + same * low1
        put(EDGE, first_sum[...])
        first_out.start()
        put(tail_at, tail_sum[...])
        tail_out.start()
        local_out(0, EDGE).start()
        local_out(OWN_BLOCKS, tail_at).start()

    for step, base in enumerate(bases):
        if step + 1 < len(bases):
            make_onehot(slots[(step + 1) % 2], bases[step + 1])
        value = scattered(slots[step % 2])
        if step == 0:
            put(0, value)
            pl.semaphore_wait(barrier, 2)
            give_lower.start()
        elif step == 1:
            put(upper_at, value)
            give_upper.start()
        elif step == 2:
            first_sum[...] = value
        elif step == 3:
            tail_sum[...] = value
        else:
            block = step - 3
            put(EDGE + block * EDGE, value)
            local_out(block, EDGE + block * EDGE).start()
        if step == 6:
            finish_edges()

    for b in range(OWN_BLOCKS):
        local_out(b, EDGE + b * EDGE).wait()
    local_out(OWN_BLOCKS, tail_at).wait()
    give_lower.wait_send()
    give_upper.wait_send()
    first_out.wait()
    tail_out.wait()


def convolve_kernel(
    region_total,
    padded,
    counts_ref,
    region_ref,
    geometry_ref,
    values_ref,
    out_ref,
    values,
    sums,
    column_at,
    line_at,
    row_at,
    kernel_even,
    kernel_odd,
    pairs,
    in_sems,
    out_sems,
):
    members, levels, _ = out_ref.shape
    me = region_ref[0]
    lower = lax.rem(me + region_total - 1, region_total)
    upper = lax.rem(me + 1, region_total)
    live = counts_ref[me]
    tail_tile = live - EDGE
    blocks = OWN_BLOCKS + 2
    tail_at = TILES_DEV + 2 * EDGE

    def tile_copy(tile):
        index = tile - EDGE
        source = jnp.where(index == tail_tile, tail_at, tile)
        source = jnp.where(index == tail_tile + 1, tail_at + 1, source)
        if tile < 2 * EDGE or tile >= EDGE + TILES_DEV:
            source = tile
        at = pl.ds((tile % EDGE) * TILE, TILE)
        return pltpu.make_async_copy(
            values_ref.at[source], values.at[tile // EDGE, :, at], in_sems.at[tile]
        )

    for tile in range(TILES_DEV + 2 * EDGE):
        tile_copy(tile).start()

    own_start = me * TILES_DEV
    starts = [lower * TILES_DEV + counts_ref[lower] - EDGE]
    starts += [own_start + b * EDGE for b in range(OWN_BLOCKS)]
    starts += [upper * TILES_DEV]
    for b in range(blocks):
        at = pl.ds(pl.multiple_of(starts[b] * TILE, TILE), BLOCK)
        shift = -1.0 if b == 0 else (1.0 if b == blocks - 1 else 0.0)
        column_at[0, b : b + 1, :] = geometry_ref[0:1, at] + shift
        column_at[1, b : b + 1, :] = geometry_ref[1:2, at]
        column_at[2, b : b + 1, :] = 0.5 * geometry_ref[2:3, at]
        for k in range(3):
            line_at[k, b, 0:1, :] = column_at[k, b : b + 1, :]

    for b in range(OWN_BLOCKS):
        for half in range(EDGE):
            at = slice(half * TILE, (half + 1) * TILE)
            for k in range(3):
                line = jnp.broadcast_to(column_at[k, b + 1 : b + 2, at], (TILE, TILE))
                row_at[k, b, at, :] = line.T

    x_all, y_all, h_all = (column_at[k, 0:blocks, :] for k in range(3))
    x_min = jnp.min(x_all, axis=1, keepdims=True)
    x_max = jnp.max(x_all, axis=1, keepdims=True)
    y_min = jnp.min(y_all, axis=1, keepdims=True)
    y_max = jnp.max(y_all, axis=1, keepdims=True)
    reach = jnp.max(h_all, axis=1, keepdims=True)
    box = [[v[b, 0] for b in range(blocks)] for v in (x_min, x_max, y_min, y_max, reach)]

    def near(i, j):
        gap_x = jnp.maximum(jnp.maximum(box[0][i] - box[1][j], box[0][j] - box[1][i]), 0.0)
        gap_y = jnp.maximum(jnp.maximum(box[2][i] - box[3][j], box[2][j] - box[3][i]), 0.0)
        most = (box[4][i] + box[4][j]) * 1.0001
        return gap_x * gap_x + gap_y * gap_y <= most * most

    count = jnp.int32(0)
    for i in range(OWN_BLOCKS):
        for j in list(range(i + 2, blocks - 1)) + [0, blocks - 1, i + 1]:
            pairs[count] = i * 16 + j
            if j == i + 1:
                count = count + 1
            else:
                use = near(i + 1, j) & (i * EDGE < live)
                if 0 < j < blocks - 1:
                    use = use & ((j - 1) * EDGE < live)
                count = count + use.astype(jnp.int32)
    pairs[count] = 1

    sums[...] = jnp.zeros_like(sums)

    def make_kernel(target, entry):
        i = lax.div(entry, 16)
        j = lax.rem(entry, 16)
        step = 64
        for half in range(EDGE):
            at = slice(half * TILE, (half + 1) * TILE)
            x, y, h = (line_at[k, j, 0:1, at] for k in range(3))
            for r in range(BLOCK // step):
                rows = slice(r * step, (r + 1) * step)
                delta_x = row_at[0, i, rows, :] - x
                delta_y = row_at[1, i, rows, :] - y
                square = delta_x * delta_x + delta_y * delta_y
                inverse = pl.reciprocal(row_at[2, i, rows, :] + h, approx=True)
                distance = square * lax.rsqrt(jnp.maximum(square, 1e-30))
                base = jnp.maximum(1.0 - distance * inverse, 0.0)
                second = base * base
                value = second * second * (5.0 - 4.0 * base)
                target[rows, at] = value.astype(jnp.bfloat16)

    def add(target, source, kernel, dims):
        product = lax.dot_general(
            values[source], kernel[...], dims, preferred_element_type=jnp.float32
        )
        for m in range(members):
            sums[target, m] += product[m * padded : m * padded + levels]

    def out_copy(i):
        at = pl.ds(pl.multiple_of(i * BLOCK, BLOCK), BLOCK)
        return pltpu.make_async_copy(sums.at[i], out_ref.at[:, :, at], out_sems.at[i])

    def work(p, now, later):
        entry = pairs[p]
        after = pairs[p + 1]
        i = lax.div(entry, 16)
        j = lax.rem(entry, 16)
        single = (j == 0) | (j == blocks - 1) | (j == i + 1)

        @pl.when(single)
        def _():
            make_kernel(later, after)
            add(i, j, now, NT)

        @pl.when(jnp.logical_not(single))
        def _():
            make_kernel(later, after)
            add(i, j, now, NT)
            add(j - 1, i + 1, now, NN)

        @pl.when(j == i + 1)
        def _():
            @pl.when((i + 1) * EDGE > live)
            def _():
                slot = lax.broadcasted_iota(jnp.int32, (levels, BLOCK), 1) + i * BLOCK
                for m in range(members):
                    sums[i, m] = jnp.where(slot < live * TILE, sums[i, m], 0.0)

            out_copy(i).start()

    make_kernel(kernel_even, pairs[0])
    for tile in range(TILES_DEV + 2 * EDGE):
        tile_copy(tile).wait()

    def two(p, carry):
        work(2 * p, kernel_even, kernel_odd)

        @pl.when(2 * p + 1 < count)
        def _():
            work(2 * p + 1, kernel_odd, kernel_even)

        return carry

    lax.fori_loop(0, lax.div(count + 1, 2), two, 0)
    for i in range(OWN_BLOCKS):
        out_copy(i).wait()


def on_device(field, stencil, weights, counts, geometry, vertical):
    members, levels, cells = field.shape
    padded = -(-levels // 16) * 16
    rows = members * padded
    region_total = lax.axis_size("reg")
    tiles = TILES_DEV + 3 * EDGE
    bf16 = jnp.bfloat16
    f32 = jnp.float32
    vmem = pl.BlockSpec(memory_space=pltpu.VMEM)
    smem = pl.BlockSpec(memory_space=pltpu.SMEM)
    anywhere = pl.BlockSpec(memory_space=pl.ANY)
    smoothed = pl.pallas_call(
        functools.partial(scatter_kernel, region_total, padded),
        out_shape=jax.ShapeDtypeStruct((tiles, rows, TILE), bf16),
        in_specs=[vmem, vmem, smem, vmem, anywhere],
        out_specs=anywhere,
        scratch_shapes=[
            pltpu.VMEM((rows, cells), bf16),
            pltpu.VMEM((2 * padded, levels), bf16),
            pltpu.VMEM((members, levels, cells), f32),
            pltpu.VMEM((BLOCK, cells), bf16),
            pltpu.VMEM((BLOCK, cells), bf16),
            pltpu.VMEM((rows, BLOCK), f32),
            pltpu.VMEM((rows, BLOCK), f32),
            pltpu.VMEM((tiles, rows, TILE), bf16),
            pltpu.VMEM((EDGE, rows, TILE), bf16),
            pltpu.VMEM((EDGE, rows, TILE), bf16),
            pltpu.SemaphoreType.DMA((cells // BLOCK,)),
            pltpu.SemaphoreType.DMA((OWN_BLOCKS + 1,)),
            pltpu.SemaphoreType.DMA((4,)),
            pltpu.SemaphoreType.DMA((4,)),
        ],
        compiler_params=pltpu.CompilerParams(
            collective_id=0, has_side_effects=True, vmem_limit_bytes=40 * 2**20
        ),
        name="scatter",
    )(stencil, weights, counts, vertical, field)
    region = lax.axis_index("reg").astype(jnp.int32).reshape(1)
    return pl.pallas_call(
        functools.partial(convolve_kernel, region_total, padded),
        out_shape=jax.ShapeDtypeStruct(field.shape, f32),
        in_specs=[smem, smem, vmem, anywhere],
        out_specs=anywhere,
        scratch_shapes=[
            pltpu.VMEM((OWN_BLOCKS + 2, rows, BLOCK), bf16),
            pltpu.VMEM((OWN_BLOCKS, members, levels, BLOCK), f32),
            pltpu.VMEM((3, 16, BLOCK), f32),
            pltpu.VMEM((3, OWN_BLOCKS + 2, 8, BLOCK), f32),
            pltpu.VMEM((3, OWN_BLOCKS, BLOCK, TILE), f32),
            pltpu.VMEM((BLOCK, BLOCK), bf16),
            pltpu.VMEM((BLOCK, BLOCK), bf16),
            pltpu.SMEM((64,), jnp.int32),
            pltpu.SemaphoreType.DMA((TILES_DEV + 2 * EDGE,)),
            pltpu.SemaphoreType.DMA((OWN_BLOCKS,)),
        ],
        compiler_params=pltpu.CompilerParams(vmem_limit_bytes=40 * 2**20),
        name="convolve",
    )(counts, region, geometry, smoothed)


def solution(mesh):
    return jax.shard_map(
        on_device,
        mesh=mesh,
        in_specs=(P("grp", None, "reg"), P(None, "reg"), P(None, "reg"), P(), P(), P()),
        out_specs=P("grp", None, "reg"),
        check_vma=False,
    )
```

```python
import functools

import jax
import jax.numpy as jnp
from jax import lax
from jax.experimental import pallas as pl
from jax.experimental.pallas import tpu as pltpu
from jax.sharding import PartitionSpec as P

TILES_DEV = 16
TILE = 128
EDGE = 2
BLOCK = EDGE * TILE
OWN_BLOCKS = TILES_DEV // EDGE
GROUP = 144
REACH = 32
MESH = pl.DeviceIdType.MESH
NT = (((1,), (1,)), ((), ()))
NN = (((1,), (0,)), ((), ()))


def scatter_kernel(
    region_total,
    padded,
    stencil_ref,
    weights_ref,
    counts_ref,
    vertical_ref,
    field_ref,
    out_ref,
    columns,
    banded,
    inputs,
    flat,
    onehot_even,
    onehot_odd,
    first_sum,
    tail_sum,
    ready,
    from_lower,
    from_upper,
    chunk_sems,
    send_sems,
    recv_sems,
):
    levels, chunks, half_rows, _ = field_ref.shape
    members = half_rows // 2
    rows = levels * members
    chunk = BLOCK
    cells = chunks * chunk
    me = lax.axis_index("reg")
    lower = lax.rem(me + region_total - 1, region_total)
    upper = lax.rem(me + 1, region_total)

    def chunk_copy(i):
        return pltpu.make_async_copy(
            field_ref.at[:, i], inputs.at[i, pl.ds(0, levels)], chunk_sems.at[i]
        )

    for i in range(chunks):
        chunk_copy(i).start()

    barrier = pltpu.get_barrier_semaphore()
    for neighbour in (lower, upper):
        pl.semaphore_signal(barrier, inc=1, device_id={"reg": neighbour}, device_id_type=MESH)

    tail_tile = counts_ref[me] - EDGE

    matrix = vertical_ref[...]
    spread = lax.broadcasted_iota(jnp.int32, (padded, levels), 0) // members
    spread = spread == lax.broadcasted_iota(jnp.int32, (padded, levels), 1)
    spread = spread.astype(jnp.float32).astype(jnp.bfloat16)
    high = matrix.astype(jnp.bfloat16)
    low = (matrix - high.astype(jnp.float32)).astype(jnp.bfloat16)
    spans = []
    for g in range(padded // GROUP):
        begin = max(g * GROUP - REACH, 0)
        end = min((g + 1) * GROUP + REACH, padded)
        spans.append((begin, end))
        mine = spread[g * GROUP : (g + 1) * GROUP]
        row = lax.broadcasted_iota(jnp.int32, (GROUP, end - begin), 0) + g * GROUP
        column = lax.broadcasted_iota(jnp.int32, (GROUP, end - begin), 1) + begin
        same = lax.rem(row, members) == lax.rem(column, members)
        for at, part in enumerate((high, low)):
            wide = jnp.dot(mine, part, preferred_element_type=jnp.float32)
            wide = lax.dot_general(
                wide.astype(jnp.bfloat16), spread[begin:end], NT,
                preferred_element_type=jnp.float32,
            )
            wide = jnp.where(same, wide, 0.0).astype(jnp.bfloat16)
            banded[g, at * GROUP : (at + 1) * GROUP, 0 : end - begin] = wide
    first_rows = lax.broadcasted_iota(jnp.int32, (half_rows, TILE), 0) < members
    for i in range(chunks):
        inputs[i, levels : levels + 1] = jnp.zeros((1, half_rows, TILE), jnp.float32)

    codes = [stencil_ref[k : k + 1, :] for k in range(3)]
    raw = [weights_ref[k : k + 1, :] for k in range(3)]
    merged = []
    for k in range(3):
        total = raw[k]
        for other in range(3):
            if other != k:
                total = total + jnp.where(codes[other] == codes[k], raw[other], 0.0)
        merged.append(total.astype(jnp.bfloat16))
    row_index = lax.broadcasted_iota(jnp.int32, (BLOCK, TILE), 0)
    row_index = row_index.astype(jnp.float32).astype(jnp.bfloat16)

    def make_onehot(target, base):
        wanted = []
        for k in range(3):
            shift = codes[k] - base
            inside = (shift >= 0) & (shift < BLOCK)
            shift = jnp.where(inside, shift, -1).astype(jnp.float32)
            wanted.append(shift.astype(jnp.bfloat16))
        for c in range(cells // TILE):
            at = slice(c * TILE, (c + 1) * TILE)
            value = jnp.zeros((BLOCK, TILE), jnp.bfloat16)
            for k in range(3):
                code = jnp.broadcast_to(wanted[k][:, at], (BLOCK, TILE))
                weight = jnp.broadcast_to(merged[k][:, at], (BLOCK, TILE))
                value = jnp.where(row_index == code, weight, value)
            target[:, at] = value

    def scattered(source):
        return lax.dot_general(
            columns[...], source[...], NT, preferred_element_type=jnp.float32
        )

    own = BLOCK
    bases = [0, BLOCK + OWN_BLOCKS * BLOCK, own, own + tail_tile * TILE]
    bases += [own + b * BLOCK for b in range(1, OWN_BLOCKS)]
    slots = [onehot_even, onehot_odd]
    make_onehot(slots[0], bases[0])

    for i in range(chunks):
        chunk_copy(i).wait()
        at = slice(i * chunk, (i + 1) * chunk)
        for p in range((levels + 1) // 2):
            even, odd = inputs[i, 2 * p], inputs[i, 2 * p + 1]
            left = jnp.where(first_rows, even, pltpu.roll(odd, members, 0))
            right = jnp.where(first_rows, pltpu.roll(even, members, 0), odd)
            both_rows = slice(p * half_rows, (p + 1) * half_rows)
            flat[both_rows, 0:TILE] = left
            flat[both_rows, TILE:] = right
        part = flat[...]
        part_high = part.astype(jnp.bfloat16)
        part_low = (part - part_high.astype(jnp.float32)).astype(jnp.bfloat16)
        for g, (begin, end) in enumerate(spans):
            weight = banded[g, :, 0 : end - begin]
            both = jnp.dot(weight, part_high[begin:end], preferred_element_type=jnp.float32)
            rest = jnp.dot(
                weight[0:GROUP], part_low[begin:end], preferred_element_type=jnp.float32
            )
            value = both[0:GROUP] + (both[GROUP : 2 * GROUP] + rest)
            columns[g * GROUP : (g + 1) * GROUP, at] = value.astype(jnp.bfloat16)

    def remote(index, source, target, neighbour):
        return pltpu.make_async_remote_copy(
            src_ref=source,
            dst_ref=target,
            send_sem=send_sems.at[index],
            recv_sem=recv_sems.at[index],
            device_id={"reg": neighbour},
            device_id_type=MESH,
        )

    upper_at = EDGE + TILES_DEV
    tail_at = upper_at + EDGE
    give_lower = remote(0, ready.at[0], from_upper, lower)
    give_upper = remote(1, ready.at[1], from_lower, upper)
    first_out = remote(2, out_ref.at[pl.ds(EDGE, EDGE)], out_ref.at[pl.ds(upper_at, EDGE)], lower)
    tail_out = remote(3, out_ref.at[pl.ds(tail_at, EDGE)], out_ref.at[pl.ds(0, EDGE)], upper)

    def put(target, tile, value):
        for half in range(EDGE):
            target[tile + half] = value[:, half * TILE : (half + 1) * TILE].astype(jnp.bfloat16)

    def finish_edges():
        give_lower.wait_recv()
        give_upper.wait_recv()
        low0, low1 = from_lower[0].astype(jnp.float32), from_lower[1].astype(jnp.float32)
        up0, up1 = from_upper[0].astype(jnp.float32), from_upper[1].astype(jnp.float32)
        same = jnp.where(tail_tile == 0, 1.0, 0.0)
        next_one = jnp.where(tail_tile == 1, 1.0, 0.0)
        first_sum[:, 0:TILE] += low0 + same * up0
        first_sum[:, TILE:] += low1 + same * up1 + next_one * up0
        tail_sum[:, 0:TILE] += up0 + same * low0 + next_one * low1
        tail_sum[:, TILE:] += up1 + same * low1
        put(out_ref, EDGE, first_sum[...])
        first_out.start()
        put(out_ref, tail_at, tail_sum[...])
        tail_out.start()

    for step, base in enumerate(bases):
        if step + 1 < len(bases):
            make_onehot(slots[(step + 1) % 2], bases[step + 1])
        value = scattered(slots[step % 2])
        if step == 0:
            put(ready.at[0], 0, value)
            pl.semaphore_wait(barrier, 2)
            give_lower.start()
        elif step == 1:
            put(ready.at[1], 0, value)
            give_upper.start()
        elif step == 2:
            first_sum[...] = value
        elif step == 3:
            tail_sum[...] = value
        else:
            block = step - 3
            put(out_ref, EDGE + block * EDGE, value)
        if step == 6:
            finish_edges()

    give_lower.wait_send()
    give_upper.wait_send()
    first_out.wait()
    tail_out.wait()


def convolve_kernel(
    region_total,
    padded,
    counts_ref,
    region_ref,
    geometry_ref,
    values_ref,
    out_ref,
    sums,
    results,
    column_at,
    line_at,
    row_at,
    kernel_even,
    kernel_odd,
    pairs,
    out_sems,
):
    levels, _, half_rows, _ = out_ref.shape
    members = half_rows // 2
    me = region_ref[0]
    lower = lax.rem(me + region_total - 1, region_total)
    upper = lax.rem(me + 1, region_total)
    live = counts_ref[me]
    tail_tile = live - EDGE
    blocks = OWN_BLOCKS + 2
    tail_at = TILES_DEV + 2 * EDGE

    def tile_values(tile):
        index = tile - EDGE
        source = jnp.where(index == tail_tile, tail_at, tile)
        source = jnp.where(index == tail_tile + 1, tail_at + 1, source)
        own = (index >= 0) & (index < TILES_DEV)
        return values_ref[jnp.where(own, source, tile)]

    def block_values(block):
        pair = [tile_values(block * EDGE + half) for half in range(EDGE)]
        return jnp.concatenate(pair, axis=1)

    own_start = me * TILES_DEV
    starts = [lower * TILES_DEV + counts_ref[lower] - EDGE]
    starts += [own_start + b * EDGE for b in range(OWN_BLOCKS)]
    starts += [upper * TILES_DEV]
    for b in range(blocks):
        at = pl.ds(pl.multiple_of(starts[b] * TILE, TILE), BLOCK)
        shift = -1.0 if b == 0 else (1.0 if b == blocks - 1 else 0.0)
        column_at[0, b : b + 1, :] = geometry_ref[0:1, at] + shift
        column_at[1, b : b + 1, :] = geometry_ref[1:2, at]
        column_at[2, b : b + 1, :] = 0.5 * geometry_ref[2:3, at]
        for k in range(3):
            line_at[k, b, 0:1, :] = column_at[k, b : b + 1, :]

    for b in range(OWN_BLOCKS):
        for half in range(EDGE):
            at = slice(half * TILE, (half + 1) * TILE)
            for k in range(3):
                line = jnp.broadcast_to(column_at[k, b + 1 : b + 2, at], (TILE, TILE))
                row_at[k, b, at, :] = line.T

    x_all, y_all, h_all = (column_at[k, 0:blocks, :] for k in range(3))
    x_min = jnp.min(x_all, axis=1, keepdims=True)
    x_max = jnp.max(x_all, axis=1, keepdims=True)
    y_min = jnp.min(y_all, axis=1, keepdims=True)
    y_max = jnp.max(y_all, axis=1, keepdims=True)
    reach = jnp.max(h_all, axis=1, keepdims=True)
    box = [[v[b, 0] for b in range(blocks)] for v in (x_min, x_max, y_min, y_max, reach)]

    def near(i, j):
        gap_x = jnp.maximum(jnp.maximum(box[0][i] - box[1][j], box[0][j] - box[1][i]), 0.0)
        gap_y = jnp.maximum(jnp.maximum(box[2][i] - box[3][j], box[2][j] - box[3][i]), 0.0)
        most = (box[4][i] + box[4][j]) * 1.0001
        return gap_x * gap_x + gap_y * gap_y <= most * most

    count = jnp.int32(0)
    for i in range(OWN_BLOCKS):
        for j in list(range(i + 2, blocks - 1)) + [0, blocks - 1, i + 1]:
            pairs[count] = i * 16 + j
            if j == i + 1:
                count = count + 1
            else:
                use = near(i + 1, j) & (i * EDGE < live)
                if 0 < j < blocks - 1:
                    use = use & ((j - 1) * EDGE < live)
                count = count + use.astype(jnp.int32)
    pairs[count] = 1

    sums[...] = jnp.zeros_like(sums)

    def make_kernel(target, entry):
        i = lax.div(entry, 16)
        j = lax.rem(entry, 16)
        step = 64
        for half in range(EDGE):
            at = slice(half * TILE, (half + 1) * TILE)
            x, y, h = (line_at[k, j, 0:1, at] for k in range(3))
            for r in range(BLOCK // step):
                rows = slice(r * step, (r + 1) * step)
                delta_x = row_at[0, i, rows, :] - x
                delta_y = row_at[1, i, rows, :] - y
                square = delta_x * delta_x + delta_y * delta_y
                inverse = pl.reciprocal(row_at[2, i, rows, :] + h, approx=True)
                distance = square * lax.rsqrt(jnp.maximum(square, 1e-30))
                base = jnp.maximum(1.0 - distance * inverse, 0.0)
                second = base * base
                value = second * second * (5.0 - 4.0 * base)
                target[rows, at] = value.astype(jnp.bfloat16)

    def add(target, source, kernel, dims):
        product = lax.dot_general(
            block_values(source), kernel[...], dims, preferred_element_type=jnp.float32
        )
        sums[target] += product

    def out_copy(i):
        return pltpu.make_async_copy(
            results.at[i, pl.ds(0, levels)], out_ref.at[:, i], out_sems.at[i]
        )

    def work(p, now, later):
        entry = pairs[p]
        after = pairs[p + 1]
        i = lax.div(entry, 16)
        j = lax.rem(entry, 16)
        single = (j == 0) | (j == blocks - 1) | (j == i + 1)

        @pl.when(single)
        def _():
            make_kernel(later, after)
            add(i, j, now, NT)

        @pl.when(jnp.logical_not(single))
        def _():
            make_kernel(later, after)
            add(i, j, now, NT)
            add(j - 1, i + 1, now, NN)

        @pl.when(j == i + 1)
        def _():
            slot = lax.broadcasted_iota(jnp.int32, (half_rows, TILE), 1) + i * BLOCK
            live_left = slot < live * TILE
            live_right = slot + TILE < live * TILE
            first_rows = lax.broadcasted_iota(jnp.int32, (half_rows, TILE), 0) < members
            for p in range((levels + 1) // 2):
                both_rows = slice(p * half_rows, (p + 1) * half_rows)
                left = jnp.where(live_left, sums[i, both_rows, 0:TILE], 0.0)
                right = jnp.where(live_right, sums[i, both_rows, TILE:], 0.0)
                results[i, 2 * p] = jnp.where(first_rows, left, pltpu.roll(right, members, 0))
                results[i, 2 * p + 1] = jnp.where(first_rows, pltpu.roll(left, members, 0), right)
            out_copy(i).start()

    make_kernel(kernel_even, pairs[0])

    def two(p, carry):
        work(2 * p, kernel_even, kernel_odd)

        @pl.when(2 * p + 1 < count)
        def _():
            work(2 * p + 1, kernel_odd, kernel_even)

        return carry

    lax.fori_loop(0, lax.div(count + 1, 2), two, 0)
    for i in range(OWN_BLOCKS):
        out_copy(i).wait()


def on_device(field, stencil, weights, counts, geometry, vertical):
    members, levels, cells = field.shape
    chunks = cells // BLOCK
    rows = -(-members * levels // GROUP) * GROUP
    half_rows = EDGE * members
    region_total = lax.axis_size("reg")
    tiles = TILES_DEV + 3 * EDGE
    bf16 = jnp.bfloat16
    f32 = jnp.float32
    vmem = pl.BlockSpec(memory_space=pltpu.VMEM)
    smem = pl.BlockSpec(memory_space=pltpu.SMEM)
    hbm = pl.BlockSpec(memory_space=pltpu.HBM)
    by_level = field.transpose(1, 0, 2).reshape(levels, members, chunks, EDGE, TILE)
    by_level = by_level.transpose(0, 2, 3, 1, 4).reshape(levels, chunks, half_rows, TILE)
    smoothed = pl.pallas_call(
        functools.partial(scatter_kernel, region_total, rows),
        out_shape=jax.ShapeDtypeStruct((tiles, rows, TILE), bf16),
        in_specs=[vmem, vmem, smem, vmem, hbm],
        out_specs=vmem,
        scratch_shapes=[
            pltpu.VMEM((rows, cells), bf16),
            pltpu.VMEM((rows // GROUP, 2 * GROUP, BLOCK), bf16),
            pltpu.VMEM((chunks, rows // members, half_rows, TILE), f32),
            pltpu.VMEM((rows, BLOCK), f32),
            pltpu.VMEM((BLOCK, cells), bf16),
            pltpu.VMEM((BLOCK, cells), bf16),
            pltpu.VMEM((rows, BLOCK), f32),
            pltpu.VMEM((rows, BLOCK), f32),
            pltpu.VMEM((2, EDGE, rows, TILE), bf16),
            pltpu.VMEM((EDGE, rows, TILE), bf16),
            pltpu.VMEM((EDGE, rows, TILE), bf16),
            pltpu.SemaphoreType.DMA((chunks,)),
            pltpu.SemaphoreType.DMA((4,)),
            pltpu.SemaphoreType.DMA((4,)),
        ],
        compiler_params=pltpu.CompilerParams(
            collective_id=0, has_side_effects=True, vmem_limit_bytes=50 * 2**20
        ),
        name="scatter",
    )(stencil, weights, counts, vertical, by_level)
    region = lax.axis_index("reg").astype(jnp.int32).reshape(1)
    result = pl.pallas_call(
        functools.partial(convolve_kernel, region_total, rows),
        out_shape=jax.ShapeDtypeStruct((levels, OWN_BLOCKS, half_rows, TILE), f32),
        in_specs=[smem, smem, vmem, vmem],
        out_specs=hbm,
        scratch_shapes=[
            pltpu.VMEM((OWN_BLOCKS, rows, BLOCK), f32),
            pltpu.VMEM((OWN_BLOCKS, rows // members, half_rows, TILE), f32),
            pltpu.VMEM((3, 16, BLOCK), f32),
            pltpu.VMEM((3, OWN_BLOCKS + 2, 8, BLOCK), f32),
            pltpu.VMEM((3, OWN_BLOCKS, BLOCK, TILE), f32),
            pltpu.VMEM((BLOCK, BLOCK), bf16),
            pltpu.VMEM((BLOCK, BLOCK), bf16),
            pltpu.SMEM((64,), jnp.int32),
            pltpu.SemaphoreType.DMA((OWN_BLOCKS,)),
        ],
        compiler_params=pltpu.CompilerParams(vmem_limit_bytes=40 * 2**20),
        name="convolve",
    )(counts, region, geometry, smoothed)
    result = result.reshape(levels, OWN_BLOCKS, EDGE, members, TILE).transpose(0, 3, 1, 2, 4)
    return result.reshape(levels, members, cells).transpose(1, 0, 2)


def solution(mesh):
    return jax.shard_map(
        on_device,
        mesh=mesh,
        in_specs=(P("grp", None, "reg"), P(None, "reg"), P(None, "reg"), P(), P(), P()),
        out_specs=P("grp", None, "reg"),
        check_vma=False,
    )
```

```python
import functools

import jax
import jax.numpy as jnp
from jax import lax
from jax.experimental import pallas as pl
from jax.experimental.pallas import tpu as pltpu
from jax.sharding import PartitionSpec as P

TILES_DEV = 16
TILE = 128
EDGE = 2
BLOCK = EDGE * TILE
OWN_BLOCKS = TILES_DEV // EDGE
GROUP = 144
REACH = 32
MESH = pl.DeviceIdType.MESH
NT = (((1,), (1,)), ((), ()))
NN = (((1,), (0,)), ((), ()))


def scatter_kernel(
    region_total,
    padded,
    stencil_ref,
    weights_ref,
    counts_ref,
    vertical_ref,
    field_ref,
    out_ref,
    columns,
    banded,
    inputs,
    flat,
    onehot_even,
    onehot_odd,
    first_sum,
    tail_sum,
    ready,
    from_lower,
    from_upper,
    chunk_sems,
    send_sems,
    recv_sems,
):
    levels, chunks, half_rows, _ = field_ref.shape
    members = half_rows // 2
    rows = levels * members
    chunk = BLOCK
    cells = chunks * chunk
    me = lax.axis_index("reg")
    lower = lax.rem(me + region_total - 1, region_total)
    upper = lax.rem(me + 1, region_total)

    def chunk_copy(i):
        return pltpu.make_async_copy(
            field_ref.at[:, i], inputs.at[i, pl.ds(0, levels)], chunk_sems.at[i]
        )

    for i in range(chunks):
        chunk_copy(i).start()

    barrier = pltpu.get_barrier_semaphore()
    for neighbour in (lower, upper):
        pl.semaphore_signal(barrier, inc=1, device_id={"reg": neighbour}, device_id_type=MESH)

    tail_tile = counts_ref[me] - EDGE

    matrix = vertical_ref[...]
    spread = lax.broadcasted_iota(jnp.int32, (padded, levels), 0) // members
    spread = spread == lax.broadcasted_iota(jnp.int32, (padded, levels), 1)
    spread = spread.astype(jnp.float32).astype(jnp.bfloat16)
    high = matrix.astype(jnp.bfloat16)
    low = (matrix - high.astype(jnp.float32)).astype(jnp.bfloat16)
    spans = []
    for g in range(padded // GROUP):
        begin = max(g * GROUP - REACH, 0)
        end = min((g + 1) * GROUP + REACH, padded)
        spans.append((begin, end))
        mine = spread[g * GROUP : (g + 1) * GROUP]
        row = lax.broadcasted_iota(jnp.int32, (GROUP, end - begin), 0) + g * GROUP
        column = lax.broadcasted_iota(jnp.int32, (GROUP, end - begin), 1) + begin
        same = lax.rem(row, members) == lax.rem(column, members)
        for at, part in enumerate((high, low)):
            wide = jnp.dot(mine, part, preferred_element_type=jnp.float32)
            wide = lax.dot_general(
                wide.astype(jnp.bfloat16), spread[begin:end], NT,
                preferred_element_type=jnp.float32,
            )
            wide = jnp.where(same, wide, 0.0).astype(jnp.bfloat16)
            banded[g, at * GROUP : (at + 1) * GROUP, 0 : end - begin] = wide
    filled = (levels + 1) // 2 * half_rows
    flat[filled:padded, :] = jnp.zeros((padded - filled, BLOCK), jnp.float32)
    first_rows = lax.broadcasted_iota(jnp.int32, (half_rows, TILE), 0) < members
    for i in range(chunks):
        inputs[i, levels : levels + 1] = jnp.zeros((1, half_rows, TILE), jnp.float32)

    codes = [stencil_ref[k : k + 1, :] for k in range(3)]
    raw = [weights_ref[k : k + 1, :] for k in range(3)]
    merged = []
    for k in range(3):
        total = raw[k]
        for other in range(3):
            if other != k:
                total = total + jnp.where(codes[other] == codes[k], raw[other], 0.0)
        merged.append(total.astype(jnp.bfloat16))
    row_index = lax.broadcasted_iota(jnp.int32, (BLOCK, TILE), 0)
    row_index = row_index.astype(jnp.float32).astype(jnp.bfloat16)

    def make_onehot(target, base):
        wanted = []
        for k in range(3):
            shift = codes[k] - base
            inside = (shift >= 0) & (shift < BLOCK)
            shift = jnp.where(inside, shift, -1).astype(jnp.float32)
            wanted.append(shift.astype(jnp.bfloat16))
        for c in range(cells // TILE):
            at = slice(c * TILE, (c + 1) * TILE)
            value = jnp.zeros((BLOCK, TILE), jnp.bfloat16)
            for k in range(3):
                code = jnp.broadcast_to(wanted[k][:, at], (BLOCK, TILE))
                weight = jnp.broadcast_to(merged[k][:, at], (BLOCK, TILE))
                value = jnp.where(row_index == code, weight, value)
            target[:, at] = value

    def scattered(source):
        return lax.dot_general(
            columns[...], source[...], NT, preferred_element_type=jnp.float32
        )

    own = BLOCK
    bases = [0, BLOCK + OWN_BLOCKS * BLOCK, own, own + tail_tile * TILE]
    bases += [own + b * BLOCK for b in range(1, OWN_BLOCKS)]
    slots = [onehot_even, onehot_odd]
    make_onehot(slots[0], bases[0])

    for i in range(chunks):
        chunk_copy(i).wait()
        at = slice(i * chunk, (i + 1) * chunk)
        for p in range((levels + 1) // 2):
            even, odd = inputs[i, 2 * p], inputs[i, 2 * p + 1]
            left = jnp.where(first_rows, even, pltpu.roll(odd, members, 0))
            right = jnp.where(first_rows, pltpu.roll(even, members, 0), odd)
            both_rows = slice(p * half_rows, (p + 1) * half_rows)
            flat[both_rows, 0:TILE] = left
            flat[both_rows, TILE:] = right
        columns[:, at] = flat[...].astype(jnp.bfloat16)

    def smooth(value):
        value_high = value.astype(jnp.bfloat16)
        value_low = (value - value_high.astype(jnp.float32)).astype(jnp.bfloat16)
        parts = []
        for g, (begin, end) in enumerate(spans):
            weight = banded[g, :, 0 : end - begin]
            both = jnp.dot(weight, value_high[begin:end], preferred_element_type=jnp.float32)
            rest = jnp.dot(
                weight[0:GROUP], value_low[begin:end], preferred_element_type=jnp.float32
            )
            parts.append(both[0:GROUP] + (both[GROUP : 2 * GROUP] + rest))
        return jnp.concatenate(parts, axis=0)

    def remote(index, source, target, neighbour):
        return pltpu.make_async_remote_copy(
            src_ref=source,
            dst_ref=target,
            send_sem=send_sems.at[index],
            recv_sem=recv_sems.at[index],
            device_id={"reg": neighbour},
            device_id_type=MESH,
        )

    upper_at = EDGE + TILES_DEV
    tail_at = upper_at + EDGE
    give_lower = remote(0, ready.at[0], from_upper, lower)
    give_upper = remote(1, ready.at[1], from_lower, upper)
    first_out = remote(2, out_ref.at[pl.ds(EDGE, EDGE)], out_ref.at[pl.ds(upper_at, EDGE)], lower)
    tail_out = remote(3, out_ref.at[pl.ds(tail_at, EDGE)], out_ref.at[pl.ds(0, EDGE)], upper)

    def put(target, tile, value):
        for half in range(EDGE):
            target[tile + half] = value[:, half * TILE : (half + 1) * TILE].astype(jnp.bfloat16)

    def finish_edges():
        give_lower.wait_recv()
        give_upper.wait_recv()
        low0, low1 = from_lower[0].astype(jnp.float32), from_lower[1].astype(jnp.float32)
        up0, up1 = from_upper[0].astype(jnp.float32), from_upper[1].astype(jnp.float32)
        same = jnp.where(tail_tile == 0, 1.0, 0.0)
        next_one = jnp.where(tail_tile == 1, 1.0, 0.0)
        first_sum[:, 0:TILE] += low0 + same * up0
        first_sum[:, TILE:] += low1 + same * up1 + next_one * up0
        tail_sum[:, 0:TILE] += up0 + same * low0 + next_one * low1
        tail_sum[:, TILE:] += up1 + same * low1
        put(out_ref, EDGE, smooth(first_sum[...]))
        first_out.start()
        put(out_ref, tail_at, smooth(tail_sum[...]))
        tail_out.start()

    for step, base in enumerate(bases):
        if step + 1 < len(bases):
            make_onehot(slots[(step + 1) % 2], bases[step + 1])
        value = scattered(slots[step % 2])
        if step == 0:
            put(ready.at[0], 0, value)
            pl.semaphore_wait(barrier, 2)
            give_lower.start()
        elif step == 1:
            put(ready.at[1], 0, value)
            give_upper.start()
        elif step == 2:
            first_sum[...] = value
        elif step == 3:
            tail_sum[...] = value
        else:
            block = step - 3
            put(out_ref, EDGE + block * EDGE, smooth(value))
        if step == 6:
            finish_edges()

    give_lower.wait_send()
    give_upper.wait_send()
    first_out.wait()
    tail_out.wait()


def convolve_kernel(
    region_total,
    padded,
    counts_ref,
    region_ref,
    geometry_ref,
    values_ref,
    out_ref,
    sums,
    results,
    column_at,
    line_at,
    row_at,
    kernel_even,
    kernel_odd,
    pairs,
    out_sems,
):
    levels, _, half_rows, _ = out_ref.shape
    members = half_rows // 2
    me = region_ref[0]
    lower = lax.rem(me + region_total - 1, region_total)
    upper = lax.rem(me + 1, region_total)
    live = counts_ref[me]
    tail_tile = live - EDGE
    blocks = OWN_BLOCKS + 2
    tail_at = TILES_DEV + 2 * EDGE

    def tile_values(tile):
        index = tile - EDGE
        source = jnp.where(index == tail_tile, tail_at, tile)
        source = jnp.where(index == tail_tile + 1, tail_at + 1, source)
        own = (index >= 0) & (index < TILES_DEV)
        return values_ref[jnp.where(own, source, tile)]

    def block_values(block):
        pair = [tile_values(block * EDGE + half) for half in range(EDGE)]
        return jnp.concatenate(pair, axis=1)

    own_start = me * TILES_DEV
    starts = [lower * TILES_DEV + counts_ref[lower] - EDGE]
    starts += [own_start + b * EDGE for b in range(OWN_BLOCKS)]
    starts += [upper * TILES_DEV]
    for b in range(blocks):
        at = pl.ds(pl.multiple_of(starts[b] * TILE, TILE), BLOCK)
        shift = -1.0 if b == 0 else (1.0 if b == blocks - 1 else 0.0)
        column_at[0, b : b + 1, :] = geometry_ref[0:1, at] + shift
        column_at[1, b : b + 1, :] = geometry_ref[1:2, at]
        column_at[2, b : b + 1, :] = 0.5 * geometry_ref[2:3, at]
        for k in range(3):
            line_at[k, b, 0:1, :] = column_at[k, b : b + 1, :]

    for b in range(OWN_BLOCKS):
        for half in range(EDGE):
            at = slice(half * TILE, (half + 1) * TILE)
            for k in range(3):
                line = jnp.broadcast_to(column_at[k, b + 1 : b + 2, at], (TILE, TILE))
                row_at[k, b, at, :] = line.T

    x_all, y_all, h_all = (column_at[k, 0:blocks, :] for k in range(3))
    x_min = jnp.min(x_all, axis=1, keepdims=True)
    x_max = jnp.max(x_all, axis=1, keepdims=True)
    y_min = jnp.min(y_all, axis=1, keepdims=True)
    y_max = jnp.max(y_all, axis=1, keepdims=True)
    reach = jnp.max(h_all, axis=1, keepdims=True)
    box = [[v[b, 0] for b in range(blocks)] for v in (x_min, x_max, y_min, y_max, reach)]

    def near(i, j):
        gap_x = jnp.maximum(jnp.maximum(box[0][i] - box[1][j], box[0][j] - box[1][i]), 0.0)
        gap_y = jnp.maximum(jnp.maximum(box[2][i] - box[3][j], box[2][j] - box[3][i]), 0.0)
        most = (box[4][i] + box[4][j]) * 1.0001
        return gap_x * gap_x + gap_y * gap_y <= most * most

    count = jnp.int32(0)
    for i in range(OWN_BLOCKS):
        for j in list(range(i + 2, blocks - 1)) + [0, blocks - 1, i + 1]:
            pairs[count] = i * 16 + j
            if j == i + 1:
                count = count + 1
            else:
                use = near(i + 1, j) & (i * EDGE < live)
                if 0 < j < blocks - 1:
                    use = use & ((j - 1) * EDGE < live)
                count = count + use.astype(jnp.int32)
    pairs[count] = 1

    sums[...] = jnp.zeros_like(sums)

    def make_kernel(target, entry):
        i = lax.div(entry, 16)
        j = lax.rem(entry, 16)
        step = 64
        for half in range(EDGE):
            at = slice(half * TILE, (half + 1) * TILE)
            x, y, h = (line_at[k, j, 0:1, at] for k in range(3))
            for r in range(BLOCK // step):
                rows = slice(r * step, (r + 1) * step)
                delta_x = row_at[0, i, rows, :] - x
                delta_y = row_at[1, i, rows, :] - y
                square = delta_x * delta_x + delta_y * delta_y
                inverse = pl.reciprocal(row_at[2, i, rows, :] + h, approx=True)
                distance = square * lax.rsqrt(jnp.maximum(square, 1e-30))
                base = jnp.maximum(1.0 - distance * inverse, 0.0)
                second = base * base
                value = second * second * (5.0 - 4.0 * base)
                target[rows, at] = value.astype(jnp.bfloat16)

    def add(target, source, kernel, dims):
        product = lax.dot_general(
            block_values(source), kernel[...], dims, preferred_element_type=jnp.float32
        )
        sums[target] += product

    def out_copy(i):
        return pltpu.make_async_copy(
            results.at[i, pl.ds(0, levels)], out_ref.at[:, i], out_sems.at[i]
        )

    def work(p, now, later):
        entry = pairs[p]
        after = pairs[p + 1]
        i = lax.div(entry, 16)
        j = lax.rem(entry, 16)
        single = (j == 0) | (j == blocks - 1) | (j == i + 1)

        @pl.when(single)
        def _():
            make_kernel(later, after)
            add(i, j, now, NT)

        @pl.when(jnp.logical_not(single))
        def _():
            make_kernel(later, after)
            add(i, j, now, NT)
            add(j - 1, i + 1, now, NN)

        @pl.when(j == i + 1)
        def _():
            slot = lax.broadcasted_iota(jnp.int32, (half_rows, TILE), 1) + i * BLOCK
            live_left = slot < live * TILE
            live_right = slot + TILE < live * TILE
            first_rows = lax.broadcasted_iota(jnp.int32, (half_rows, TILE), 0) < members
            for p in range((levels + 1) // 2):
                both_rows = slice(p * half_rows, (p + 1) * half_rows)
                left = jnp.where(live_left, sums[i, both_rows, 0:TILE], 0.0)
                right = jnp.where(live_right, sums[i, both_rows, TILE:], 0.0)
                results[i, 2 * p] = jnp.where(first_rows, left, pltpu.roll(right, members, 0))
                results[i, 2 * p + 1] = jnp.where(first_rows, pltpu.roll(left, members, 0), right)
            out_copy(i).start()

    make_kernel(kernel_even, pairs[0])

    def two(p, carry):
        work(2 * p, kernel_even, kernel_odd)

        @pl.when(2 * p + 1 < count)
        def _():
            work(2 * p + 1, kernel_odd, kernel_even)

        return carry

    lax.fori_loop(0, lax.div(count + 1, 2), two, 0)
    for i in range(OWN_BLOCKS):
        out_copy(i).wait()


def on_device(field, stencil, weights, counts, geometry, vertical):
    members, levels, cells = field.shape
    chunks = cells // BLOCK
    rows = -(-members * levels // GROUP) * GROUP
    half_rows = EDGE * members
    region_total = lax.axis_size("reg")
    tiles = TILES_DEV + 3 * EDGE
    bf16 = jnp.bfloat16
    f32 = jnp.float32
    vmem = pl.BlockSpec(memory_space=pltpu.VMEM)
    smem = pl.BlockSpec(memory_space=pltpu.SMEM)
    hbm = pl.BlockSpec(memory_space=pltpu.HBM)
    by_level = field.transpose(1, 0, 2).reshape(levels, members, chunks, EDGE, TILE)
    by_level = by_level.transpose(0, 2, 3, 1, 4).reshape(levels, chunks, half_rows, TILE)
    smoothed = pl.pallas_call(
        functools.partial(scatter_kernel, region_total, rows),
        out_shape=jax.ShapeDtypeStruct((tiles, rows, TILE), bf16),
        in_specs=[vmem, vmem, smem, vmem, hbm],
        out_specs=vmem,
        scratch_shapes=[
            pltpu.VMEM((rows, cells), bf16),
            pltpu.VMEM((rows // GROUP, 2 * GROUP, BLOCK), bf16),
            pltpu.VMEM((chunks, rows // members, half_rows, TILE), f32),
            pltpu.VMEM((rows, BLOCK), f32),
            pltpu.VMEM((BLOCK, cells), bf16),
            pltpu.VMEM((BLOCK, cells), bf16),
            pltpu.VMEM((rows, BLOCK), f32),
            pltpu.VMEM((rows, BLOCK), f32),
            pltpu.VMEM((2, EDGE, rows, TILE), bf16),
            pltpu.VMEM((EDGE, rows, TILE), bf16),
            pltpu.VMEM((EDGE, rows, TILE), bf16),
            pltpu.SemaphoreType.DMA((chunks,)),
            pltpu.SemaphoreType.DMA((4,)),
            pltpu.SemaphoreType.DMA((4,)),
        ],
        compiler_params=pltpu.CompilerParams(
            collective_id=0, has_side_effects=True, vmem_limit_bytes=50 * 2**20
        ),
        name="scatter",
    )(stencil, weights, counts, vertical, by_level)
    region = lax.axis_index("reg").astype(jnp.int32).reshape(1)
    result = pl.pallas_call(
        functools.partial(convolve_kernel, region_total, rows),
        out_shape=jax.ShapeDtypeStruct((levels, OWN_BLOCKS, half_rows, TILE), f32),
        in_specs=[smem, smem, vmem, vmem],
        out_specs=hbm,
        scratch_shapes=[
            pltpu.VMEM((OWN_BLOCKS, rows, BLOCK), f32),
            pltpu.VMEM((OWN_BLOCKS, rows // members, half_rows, TILE), f32),
            pltpu.VMEM((3, 16, BLOCK), f32),
            pltpu.VMEM((3, OWN_BLOCKS + 2, 8, BLOCK), f32),
            pltpu.VMEM((3, OWN_BLOCKS, BLOCK, TILE), f32),
            pltpu.VMEM((BLOCK, BLOCK), bf16),
            pltpu.VMEM((BLOCK, BLOCK), bf16),
            pltpu.SMEM((64,), jnp.int32),
            pltpu.SemaphoreType.DMA((OWN_BLOCKS,)),
        ],
        compiler_params=pltpu.CompilerParams(vmem_limit_bytes=40 * 2**20),
        name="convolve",
    )(counts, region, geometry, smoothed)
    result = result.reshape(levels, OWN_BLOCKS, EDGE, members, TILE).transpose(0, 3, 1, 2, 4)
    return result.reshape(levels, members, cells).transpose(1, 0, 2)


def solution(mesh):
    return jax.shard_map(
        on_device,
        mesh=mesh,
        in_specs=(P("grp", None, "reg"), P(None, "reg"), P(None, "reg"), P(), P(), P()),
        out_specs=P("grp", None, "reg"),
        check_vma=False,
    )
```

```python
import functools

import jax
import jax.numpy as jnp
from jax import lax
from jax.experimental import pallas as pl
from jax.experimental.pallas import tpu as pltpu
from jax.sharding import PartitionSpec as P

TILES_DEV = 16
TILE = 128
EDGE = 2
BLOCK = EDGE * TILE
OWN_BLOCKS = TILES_DEV // EDGE
GROUP = 144
REACH = 32
MESH = pl.DeviceIdType.MESH
NT = (((1,), (1,)), ((), ()))
NN = (((1,), (0,)), ((), ()))


def scatter_kernel(
    region_total,
    padded,
    stencil_ref,
    weights_ref,
    counts_ref,
    vertical_ref,
    field_ref,
    out_ref,
    columns,
    banded,
    inputs,
    flat,
    onehot_even,
    onehot_odd,
    first_sum,
    tail_sum,
    ready,
    from_lower,
    from_upper,
    chunk_sems,
    send_sems,
    recv_sems,
):
    levels, chunks, half_rows, _ = field_ref.shape
    members = half_rows // 2
    rows = levels * members
    chunk = BLOCK
    cells = chunks * chunk
    me = lax.axis_index("reg")
    lower = lax.rem(me + region_total - 1, region_total)
    upper = lax.rem(me + 1, region_total)

    def chunk_copy(i):
        return pltpu.make_async_copy(
            field_ref.at[:, i], inputs.at[i, pl.ds(0, levels)], chunk_sems.at[i]
        )

    for i in range(chunks):
        chunk_copy(i).start()

    barrier = pltpu.get_barrier_semaphore()
    for neighbour in (lower, upper):
        pl.semaphore_signal(barrier, inc=1, device_id={"reg": neighbour}, device_id_type=MESH)

    tail_tile = counts_ref[me] - EDGE

    matrix = vertical_ref[...]
    spread = lax.broadcasted_iota(jnp.int32, (padded, levels), 0) // members
    spread = spread == lax.broadcasted_iota(jnp.int32, (padded, levels), 1)
    spread = spread.astype(jnp.float32).astype(jnp.bfloat16)
    high = matrix.astype(jnp.bfloat16)
    low = (matrix - high.astype(jnp.float32)).astype(jnp.bfloat16)
    spans = []
    for g in range(padded // GROUP):
        begin = max(g * GROUP - REACH, 0)
        end = min((g + 1) * GROUP + REACH, padded)
        spans.append((begin, end))
        mine = spread[g * GROUP : (g + 1) * GROUP]
        row = lax.broadcasted_iota(jnp.int32, (GROUP, end - begin), 0) + g * GROUP
        column = lax.broadcasted_iota(jnp.int32, (GROUP, end - begin), 1) + begin
        same = lax.rem(row, members) == lax.rem(column, members)
        for at, part in enumerate((high, low)):
            wide = jnp.dot(mine, part, preferred_element_type=jnp.float32)
            wide = lax.dot_general(
                wide.astype(jnp.bfloat16), spread[begin:end], NT,
                preferred_element_type=jnp.float32,
            )
            wide = jnp.where(same, wide, 0.0).astype(jnp.bfloat16)
            banded[g, at * GROUP : (at + 1) * GROUP, 0 : end - begin] = wide
    filled = (levels + 1) // 2 * half_rows
    flat[filled:padded, :] = jnp.zeros((padded - filled, BLOCK), jnp.float32)
    first_rows = lax.broadcasted_iota(jnp.int32, (half_rows, TILE), 0) < members
    for i in range(chunks):
        inputs[i, levels : levels + 1] = jnp.zeros((1, half_rows, TILE), jnp.float32)

    codes = [stencil_ref[k : k + 1, :] for k in range(3)]
    raw = [weights_ref[k : k + 1, :] for k in range(3)]
    merged = []
    for k in range(3):
        total = raw[k]
        for other in range(3):
            if other != k:
                total = total + jnp.where(codes[other] == codes[k], raw[other], 0.0)
        merged.append(total.astype(jnp.bfloat16))
    row_index = lax.broadcasted_iota(jnp.int32, (BLOCK, TILE), 0)
    row_index = row_index.astype(jnp.float32).astype(jnp.bfloat16)

    def make_onehot(target, base):
        wanted = []
        for k in range(3):
            shift = codes[k] - base
            inside = (shift >= 0) & (shift < BLOCK)
            shift = jnp.where(inside, shift, -1).astype(jnp.float32)
            wanted.append(shift.astype(jnp.bfloat16))
        for c in range(cells // TILE):
            at = slice(c * TILE, (c + 1) * TILE)
            value = jnp.zeros((BLOCK, TILE), jnp.bfloat16)
            for k in range(3):
                code = jnp.broadcast_to(wanted[k][:, at], (BLOCK, TILE))
                weight = jnp.broadcast_to(merged[k][:, at], (BLOCK, TILE))
                value = jnp.where(row_index == code, weight, value)
            target[:, at] = value

    def scattered(source):
        return lax.dot_general(
            columns[...], source[...], NT, preferred_element_type=jnp.float32
        )

    own = BLOCK
    bases = [0, BLOCK + OWN_BLOCKS * BLOCK, own, own + tail_tile * TILE]
    bases += [own + b * BLOCK for b in range(1, OWN_BLOCKS)]
    slots = [onehot_even, onehot_odd]
    make_onehot(slots[0], bases[0])

    for i in range(chunks):
        chunk_copy(i).wait()
        at = slice(i * chunk, (i + 1) * chunk)
        for p in range((levels + 1) // 2):
            even, odd = inputs[i, 2 * p], inputs[i, 2 * p + 1]
            left = jnp.where(first_rows, even, pltpu.roll(odd, members, 0))
            right = jnp.where(first_rows, pltpu.roll(even, members, 0), odd)
            both_rows = slice(p * half_rows, (p + 1) * half_rows)
            flat[both_rows, 0:TILE] = left
            flat[both_rows, TILE:] = right
        columns[:, at] = flat[...].astype(jnp.bfloat16)

    def smooth(value):
        value_high = value.astype(jnp.bfloat16)
        value_low = (value - value_high.astype(jnp.float32)).astype(jnp.bfloat16)
        parts = []
        for g, (begin, end) in enumerate(spans):
            weight = banded[g, :, 0 : end - begin]
            both = jnp.dot(weight, value_high[begin:end], preferred_element_type=jnp.float32)
            rest = jnp.dot(
                weight[0:GROUP], value_low[begin:end], preferred_element_type=jnp.float32
            )
            parts.append(both[0:GROUP] + (both[GROUP : 2 * GROUP] + rest))
        return jnp.concatenate(parts, axis=0)

    def remote(index, source, target, neighbour):
        return pltpu.make_async_remote_copy(
            src_ref=source,
            dst_ref=target,
            send_sem=send_sems.at[index],
            recv_sem=recv_sems.at[index],
            device_id={"reg": neighbour},
            device_id_type=MESH,
        )

    upper_at = EDGE + TILES_DEV
    tail_at = upper_at + EDGE
    give_lower = remote(0, ready.at[0], from_upper, lower)
    give_upper = remote(1, ready.at[1], from_lower, upper)
    first_out = remote(2, out_ref.at[pl.ds(EDGE, EDGE)], out_ref.at[pl.ds(upper_at, EDGE)], lower)
    tail_out = remote(3, out_ref.at[pl.ds(tail_at, EDGE)], out_ref.at[pl.ds(0, EDGE)], upper)

    def put(target, tile, value):
        for half in range(EDGE):
            target[tile + half] = value[:, half * TILE : (half + 1) * TILE].astype(jnp.bfloat16)

    def finish_edges():
        give_lower.wait_recv()
        give_upper.wait_recv()
        low0, low1 = from_lower[0].astype(jnp.float32), from_lower[1].astype(jnp.float32)
        up0, up1 = from_upper[0].astype(jnp.float32), from_upper[1].astype(jnp.float32)
        same = jnp.where(tail_tile == 0, 1.0, 0.0)
        next_one = jnp.where(tail_tile == 1, 1.0, 0.0)
        first_sum[:, 0:TILE] += low0 + same * up0
        first_sum[:, TILE:] += low1 + same * up1 + next_one * up0
        tail_sum[:, 0:TILE] += up0 + same * low0 + next_one * low1
        tail_sum[:, TILE:] += up1 + same * low1
        put(out_ref, EDGE, smooth(first_sum[...]))
        first_out.start()
        put(out_ref, tail_at, smooth(tail_sum[...]))
        tail_out.start()

    for step, base in enumerate(bases):
        if step + 1 < len(bases):
            make_onehot(slots[(step + 1) % 2], bases[step + 1])
        value = scattered(slots[step % 2])
        if step == 0:
            put(ready.at[0], 0, value)
            pl.semaphore_wait(barrier, 2)
            give_lower.start()
        elif step == 1:
            put(ready.at[1], 0, value)
            give_upper.start()
        elif step == 2:
            first_sum[...] = value
        elif step == 3:
            tail_sum[...] = value
        else:
            block = step - 3
            put(out_ref, EDGE + block * EDGE, smooth(value))
        if step == 4:
            finish_edges()

    give_lower.wait_send()
    give_upper.wait_send()
    first_out.wait()
    tail_out.wait()


def convolve_kernel(
    region_total,
    padded,
    counts_ref,
    region_ref,
    geometry_ref,
    values_ref,
    out_ref,
    sums,
    results,
    column_at,
    line_at,
    row_at,
    kernel_even,
    kernel_odd,
    pairs,
    out_sems,
):
    levels, _, half_rows, _ = out_ref.shape
    members = half_rows // 2
    me = region_ref[0]
    lower = lax.rem(me + region_total - 1, region_total)
    upper = lax.rem(me + 1, region_total)
    live = counts_ref[me]
    tail_tile = live - EDGE
    blocks = OWN_BLOCKS + 2
    tail_at = TILES_DEV + 2 * EDGE

    def tile_values(tile):
        index = tile - EDGE
        source = jnp.where(index == tail_tile, tail_at, tile)
        source = jnp.where(index == tail_tile + 1, tail_at + 1, source)
        own = (index >= 0) & (index < TILES_DEV)
        return values_ref[jnp.where(own, source, tile)]

    def block_values(block):
        pair = [tile_values(block * EDGE + half) for half in range(EDGE)]
        return jnp.concatenate(pair, axis=1)

    own_start = me * TILES_DEV
    starts = [lower * TILES_DEV + counts_ref[lower] - EDGE]
    starts += [own_start + b * EDGE for b in range(OWN_BLOCKS)]
    starts += [upper * TILES_DEV]
    for b in range(blocks):
        at = pl.ds(pl.multiple_of(starts[b] * TILE, TILE), BLOCK)
        shift = -1.0 if b == 0 else (1.0 if b == blocks - 1 else 0.0)
        column_at[0, b : b + 1, :] = geometry_ref[0:1, at] + shift
        column_at[1, b : b + 1, :] = geometry_ref[1:2, at]
        column_at[2, b : b + 1, :] = 0.5 * geometry_ref[2:3, at]
        for k in range(3):
            line_at[k, b, 0:1, :] = column_at[k, b : b + 1, :]

    for b in range(OWN_BLOCKS):
        for half in range(EDGE):
            at = slice(half * TILE, (half + 1) * TILE)
            for k in range(3):
                line = jnp.broadcast_to(column_at[k, b + 1 : b + 2, at], (TILE, TILE))
                row_at[k, b, at, :] = line.T

    x_all, y_all, h_all = (column_at[k, 0:blocks, :] for k in range(3))
    x_min = jnp.min(x_all, axis=1, keepdims=True)
    x_max = jnp.max(x_all, axis=1, keepdims=True)
    y_min = jnp.min(y_all, axis=1, keepdims=True)
    y_max = jnp.max(y_all, axis=1, keepdims=True)
    reach = jnp.max(h_all, axis=1, keepdims=True)
    box = [[v[b, 0] for b in range(blocks)] for v in (x_min, x_max, y_min, y_max, reach)]

    def near(i, j):
        gap_x = jnp.maximum(jnp.maximum(box[0][i] - box[1][j], box[0][j] - box[1][i]), 0.0)
        gap_y = jnp.maximum(jnp.maximum(box[2][i] - box[3][j], box[2][j] - box[3][i]), 0.0)
        most = (box[4][i] + box[4][j]) * 1.0001
        return gap_x * gap_x + gap_y * gap_y <= most * most

    count = jnp.int32(0)
    for i in range(OWN_BLOCKS):
        for j in list(range(i + 2, blocks - 1)) + [0, blocks - 1, i + 1]:
            pairs[count] = i * 16 + j
            if j == i + 1:
                count = count + 1
            else:
                use = near(i + 1, j) & (i * EDGE < live)
                if 0 < j < blocks - 1:
                    use = use & ((j - 1) * EDGE < live)
                count = count + use.astype(jnp.int32)
    pairs[count] = 1

    sums[...] = jnp.zeros_like(sums)

    def make_kernel(target, entry):
        i = lax.div(entry, 16)
        j = lax.rem(entry, 16)
        step = 64
        for half in range(EDGE):
            at = slice(half * TILE, (half + 1) * TILE)
            x, y, h = (line_at[k, j, 0:1, at] for k in range(3))
            for r in range(BLOCK // step):
                rows = slice(r * step, (r + 1) * step)
                delta_x = row_at[0, i, rows, :] - x
                delta_y = row_at[1, i, rows, :] - y
                square = delta_x * delta_x + delta_y * delta_y
                inverse = pl.reciprocal(row_at[2, i, rows, :] + h, approx=True)
                distance = square * lax.rsqrt(jnp.maximum(square, 1e-30))
                base = jnp.maximum(1.0 - distance * inverse, 0.0)
                second = base * base
                value = second * second * (5.0 - 4.0 * base)
                target[rows, at] = value.astype(jnp.bfloat16)

    def add(target, source, kernel, dims):
        product = lax.dot_general(
            block_values(source), kernel[...], dims, preferred_element_type=jnp.float32
        )
        sums[target] += product

    def out_copy(i):
        return pltpu.make_async_copy(
            results.at[i, pl.ds(0, levels)], out_ref.at[:, i], out_sems.at[i]
        )

    def work(p, now, later):
        entry = pairs[p]
        after = pairs[p + 1]
        i = lax.div(entry, 16)
        j = lax.rem(entry, 16)
        single = (j == 0) | (j == blocks - 1) | (j == i + 1)

        @pl.when(single)
        def _():
            make_kernel(later, after)
            add(i, j, now, NT)

        @pl.when(jnp.logical_not(single))
        def _():
            make_kernel(later, after)
            add(i, j, now, NT)
            add(j - 1, i + 1, now, NN)

        @pl.when(j == i + 1)
        def _():
            slot = lax.broadcasted_iota(jnp.int32, (half_rows, TILE), 1) + i * BLOCK
            live_left = slot < live * TILE
            live_right = slot + TILE < live * TILE
            first_rows = lax.broadcasted_iota(jnp.int32, (half_rows, TILE), 0) < members
            for p in range((levels + 1) // 2):
                both_rows = slice(p * half_rows, (p + 1) * half_rows)
                left = jnp.where(live_left, sums[i, both_rows, 0:TILE], 0.0)
                right = jnp.where(live_right, sums[i, both_rows, TILE:], 0.0)
                results[i, 2 * p] = jnp.where(first_rows, left, pltpu.roll(right, members, 0))
                results[i, 2 * p + 1] = jnp.where(first_rows, pltpu.roll(left, members, 0), right)
            out_copy(i).start()

    make_kernel(kernel_even, pairs[0])

    def two(p, carry):
        work(2 * p, kernel_even, kernel_odd)

        @pl.when(2 * p + 1 < count)
        def _():
            work(2 * p + 1, kernel_odd, kernel_even)

        return carry

    lax.fori_loop(0, lax.div(count + 1, 2), two, 0)
    for i in range(OWN_BLOCKS):
        out_copy(i).wait()


def on_device(field, stencil, weights, counts, geometry, vertical):
    members, levels, cells = field.shape
    chunks = cells // BLOCK
    rows = -(-members * levels // GROUP) * GROUP
    half_rows = EDGE * members
    region_total = lax.axis_size("reg")
    tiles = TILES_DEV + 3 * EDGE
    bf16 = jnp.bfloat16
    f32 = jnp.float32
    vmem = pl.BlockSpec(memory_space=pltpu.VMEM)
    smem = pl.BlockSpec(memory_space=pltpu.SMEM)
    hbm = pl.BlockSpec(memory_space=pltpu.HBM)
    by_level = field.transpose(1, 0, 2).reshape(levels, members, chunks, EDGE, TILE)
    by_level = by_level.transpose(0, 2, 3, 1, 4).reshape(levels, chunks, half_rows, TILE)
    smoothed = pl.pallas_call(
        functools.partial(scatter_kernel, region_total, rows),
        out_shape=jax.ShapeDtypeStruct((tiles, rows, TILE), bf16),
        in_specs=[vmem, vmem, smem, vmem, hbm],
        out_specs=vmem,
        scratch_shapes=[
            pltpu.VMEM((rows, cells), bf16),
            pltpu.VMEM((rows // GROUP, 2 * GROUP, BLOCK), bf16),
            pltpu.VMEM((chunks, rows // members, half_rows, TILE), f32),
            pltpu.VMEM((rows, BLOCK), f32),
            pltpu.VMEM((BLOCK, cells), bf16),
            pltpu.VMEM((BLOCK, cells), bf16),
            pltpu.VMEM((rows, BLOCK), f32),
            pltpu.VMEM((rows, BLOCK), f32),
            pltpu.VMEM((2, EDGE, rows, TILE), bf16),
            pltpu.VMEM((EDGE, rows, TILE), bf16),
            pltpu.VMEM((EDGE, rows, TILE), bf16),
            pltpu.SemaphoreType.DMA((chunks,)),
            pltpu.SemaphoreType.DMA((4,)),
            pltpu.SemaphoreType.DMA((4,)),
        ],
        compiler_params=pltpu.CompilerParams(
            collective_id=0, has_side_effects=True, vmem_limit_bytes=50 * 2**20
        ),
        name="scatter",
    )(stencil, weights, counts, vertical, by_level)
    region = lax.axis_index("reg").astype(jnp.int32).reshape(1)
    result = pl.pallas_call(
        functools.partial(convolve_kernel, region_total, rows),
        out_shape=jax.ShapeDtypeStruct((levels, OWN_BLOCKS, half_rows, TILE), f32),
        in_specs=[smem, smem, vmem, vmem],
        out_specs=hbm,
        scratch_shapes=[
            pltpu.VMEM((OWN_BLOCKS, rows, BLOCK), f32),
            pltpu.VMEM((OWN_BLOCKS, rows // members, half_rows, TILE), f32),
            pltpu.VMEM((3, 16, BLOCK), f32),
            pltpu.VMEM((3, OWN_BLOCKS + 2, 8, BLOCK), f32),
            pltpu.VMEM((3, OWN_BLOCKS, BLOCK, TILE), f32),
            pltpu.VMEM((BLOCK, BLOCK), bf16),
            pltpu.VMEM((BLOCK, BLOCK), bf16),
            pltpu.SMEM((64,), jnp.int32),
            pltpu.SemaphoreType.DMA((OWN_BLOCKS,)),
        ],
        compiler_params=pltpu.CompilerParams(vmem_limit_bytes=40 * 2**20),
        name="convolve",
    )(counts, region, geometry, smoothed)
    result = result.reshape(levels, OWN_BLOCKS, EDGE, members, TILE).transpose(0, 3, 1, 2, 4)
    return result.reshape(levels, members, cells).transpose(1, 0, 2)


def solution(mesh):
    return jax.shard_map(
        on_device,
        mesh=mesh,
        in_specs=(P("grp", None, "reg"), P(None, "reg"), P(None, "reg"), P(), P(), P()),
        out_specs=P("grp", None, "reg"),
        check_vma=False,
    )
```
